256 devices in a mesh: ub: 16 (over y, x), ib: 16 (over z, core).
Axes of the slice: x: 4, y: 4, z: 8, core: 2. Of those that a mesh axis runs over, the one named last changes fastest.
Arguments:
- user_factors: bfloat16 [65536, 256], P(('ub', 'ib')), may hold values from -80 to 80
- item_factors: float32 [8192, 256], P('ib'), may hold values from -3 to 3
- tile_rows: int32 [16, 16, 16], P('ub', 'ib'), may hold values from 0 to 31, as said below
- tile_cols: int32 [16, 16, 16], P('ub', 'ib'), may hold values from 0 to 3
- tile_count: int32 [16, 16], P('ub', 'ib'), may hold values from 1 to 16, as said below
- tile_weights: bfloat16 [16, 16, 16, 128, 128], P('ub', 'ib'), may hold values from 0 to 4, as said below
Outputs:
- updated_factors: float32 [8192, 256], P('ib')
The draws below stay inside these ranges and needn't reach their ends.
Inputs may be any that keep to these rules, and one draw needn't show every extreme that they name: `tile_rows`: the 16 slots of one device name distinct (user block, item block) pairs, taken with tile_cols. Only the first tile_count slots of a device are live; the other slots hold stale blocks and weights. `tile_weights`: zero where a pair is not observed, else the pair's confidence weight.
All inputs are finite; a program needn't handle non-finite values.
Results may differ from the reference program's by a relative error of at most 0.0045.
Values may be sent and summed in bfloat16 or wider, within the bound.
No kernel may reach another device: no remote copies, remote signals or barrier semaphores. Data moves between devices by JAX's collectives and lax.ppermute only.
A program may use at most 64 MiB of HBM per device.

```python
import math
import jax
import jax.numpy as jnp
from jax import lax

K = 256
TILE = 128
ITERS = 4
IB_BLK = 4
NT = 16
USERS = 65536
UBS = 32
ITEMS = 8192
N_UB = 16
N_IB = 16


def tile_pairs(key):
    device_keys = jax.random.split(jax.random.fold_in(key, 5), N_UB * N_IB)
    picked = jax.vmap(lambda single: jax.random.permutation(single, UBS * IB_BLK)[:NT])(device_keys)
    return picked.reshape(N_UB, N_IB, NT).astype(jnp.int32)


def draw_tile_rows(key, part):
    return (tile_pairs(key) // IB_BLK).astype(jnp.int32)


def draw_tile_cols(key, part):
    return (tile_pairs(key) % IB_BLK).astype(jnp.int32)


def draw_tile_count(key, part):
    key = jax.random.fold_in(key, 31)
    first_key, second_key, third_key = jax.random.split(key, 3)
    grid_shape = (N_UB, N_IB)
    factor_one = jax.random.randint(first_key, grid_shape, NT // 2, NT + 1)
    factor_two = jax.random.randint(second_key, grid_shape, 1, NT + 1)
    counts = jnp.maximum(1, factor_one * factor_two // NT)
    chosen = jax.random.randint(third_key, (), 0, N_UB * N_IB)
    flat_index = jnp.arange(N_UB * N_IB).reshape(grid_shape)
    return jnp.where(flat_index == chosen, NT, counts).astype(jnp.int32)


def draw_tile_weights(key, part):
    key = jax.random.fold_in(key, 41)
    mask_key, level_key = jax.random.split(key)
    grid_shape = (N_UB, N_IB, NT, TILE, TILE)
    observed = jax.random.randint(mask_key, grid_shape, 0, 5) < 2
    levels = jnp.exp(jax.random.uniform(level_key, grid_shape, jnp.float32, math.log(0.5), math.log(4.0)))
    return jnp.where(observed, levels, 0.0).astype(jnp.bfloat16)


def draw_user_factors(key, part):
    key = jax.random.fold_in(key, 17)
    base_key, row_key, col_key = jax.random.split(key, 3)
    index_ramp = 1.0 + 2.0 * jnp.arange(USERS, dtype=jnp.float32)[:, None] / (USERS - 1)
    col_scale = jnp.exp(jax.random.uniform(col_key, (1, K), jnp.float32, 0.0, math.log(8.0)))
    base_values = jnp.clip(jax.random.normal(base_key, (USERS, K), jnp.float32), -4.0, 4.0)
    row_scale = jnp.exp(jax.random.uniform(row_key, (USERS, 1), jnp.float32, 0.0, math.log(3.3)))
    return (0.08 * base_values * row_scale * index_ramp * col_scale).astype(jnp.bfloat16)


def level_of(stream_key, dims, shards, low, top_value):
    gain = 1.0
    for dim, shards_of in shards:
        draws = jax.random.uniform(jax.random.fold_in(jax.random.fold_in(stream_key, 6), dim), (shards_of,), jnp.float32, low / len(shards), top_value / len(shards))
        gain = gain * jnp.repeat(jnp.exp(draws), dims[dim] // shards_of).reshape((-1,) + (1,) * (len(dims) - 1 - dim))
    return gain


def normal_values(own_key, extent, spread, most, cuts=(), kind=jnp.bfloat16):
    factor_of = level_of(own_key, extent, cuts, -0.22, 0.18) if cuts else 1.0
    result = jax.random.normal(own_key, extent, jnp.float32) * spread * factor_of
    return jnp.minimum(jnp.maximum(result, -most), most).astype(kind)


def setup_inputs(seed: int = 0) -> dict:
    seeds = jax.random.split(jax.random.key(seed), 7)
    return {
        "user_factors": draw_user_factors(jax.random.fold_in(seeds[6], 71), 0),
        "item_factors": normal_values(seeds[1], (ITEMS, K), 0.5, 3.0, ((0, 16),), jnp.float32),
        "tile_rows": draw_tile_rows(jax.random.fold_in(seeds[6], 71), 0),
        "tile_cols": draw_tile_cols(jax.random.fold_in(seeds[6], 71), 0),
        "tile_count": draw_tile_count(jax.random.fold_in(seeds[6], 71), 0),
        "tile_weights": draw_tile_weights(jax.random.fold_in(seeds[6], 71), 0),
    }


UNOBSERVED = 1024.0
PENALTY = 8.0
EPSILON = 1e-6
finest = lax.Precision.HIGHEST


def reference(user_factors, item_factors, tile_rows, tile_cols, tile_count, tile_weights):
    user_rows = user_factors.astype(jnp.float32)
    gram_matrix = jnp.dot(user_rows.T, user_rows, precision=finest) * (UNOBSERVED / USERS)
    panels = user_rows.reshape(N_UB, UBS, TILE, K)
    half_width = K // 2
    column_data = (item_factors.reshape(N_IB, IB_BLK * TILE, K),
                   jnp.swapaxes(tile_rows, 0, 1), jnp.swapaxes(tile_cols, 0, 1),
                   jnp.swapaxes(tile_count, 0, 1), jnp.swapaxes(tile_weights, 0, 1))

    def column(inputs):
        factors, block_ids, target_ids, live_count, weights = inputs
        user_tiles = jax.vmap(lambda block_table, picked: block_table[picked])(panels, block_ids)
        live_mask = (jnp.arange(NT)[None, :] < live_count[:, None]).astype(jnp.float32)
        owner_map = (target_ids[:, :, None] == jnp.arange(IB_BLK)[None, None, :]).astype(jnp.float32) * live_mask[:, :, None]
        confidence = weights.astype(jnp.float32)

        def gather_tiles(vector, width):
            return vector.reshape(IB_BLK, TILE, width)[target_ids]

        def collect(pulled):
            return jnp.einsum("ptb,ptid->bid", owner_map, pulled, precision=finest).reshape(IB_BLK * TILE, -1)

        predicted = jnp.einsum("ptud,ptid->ptui", user_tiles, gather_tiles(factors, K), precision=finest)
        for block_index in range(2):
            first_col = block_index * half_width
            user_half = user_tiles[..., first_col:first_col + half_width]
            gram_cols = gram_matrix[:, first_col:first_col + half_width]
            gram_block = gram_matrix[first_col:first_col + half_width, first_col:first_col + half_width]
            pulled = jnp.einsum("ptui,ptud->ptid", confidence * (predicted - 1.0), user_half, precision=finest)
            gradient = collect(pulled) + jnp.dot(factors, gram_cols, precision=finest) + PENALTY * factors[:, first_col:first_col + half_width]
            residual = -gradient
            direction = residual
            norm_sq = jnp.sum(residual * residual, axis=1, keepdims=True)
            update = jnp.zeros_like(residual)
            for round_index in range(ITERS):
                inner_vals = jnp.einsum("ptud,ptid->ptui", user_half, gather_tiles(direction, half_width), precision=finest)
                pulled = jnp.einsum("ptui,ptud->ptid", confidence * inner_vals, user_half, precision=finest)
                applied = collect(pulled) + jnp.dot(direction, gram_block, precision=finest) + PENALTY * direction
                step_size = norm_sq / (jnp.sum(direction * applied, axis=1, keepdims=True) + EPSILON)
                update = update + step_size * direction
                residual = residual - step_size * applied
                if round_index + 1 < ITERS:
                    norm_next = jnp.sum(residual * residual, axis=1, keepdims=True)
                    direction = residual + (norm_next / (norm_sq + EPSILON)) * direction
                    norm_sq = norm_next
            factors = factors.at[:, first_col:first_col + half_width].add(update)
            if block_index == 0:
                predicted = predicted + jnp.einsum("ptud,ptid->ptui", user_half, gather_tiles(update, half_width), precision=finest)
        return factors

    return lax.map(column, column_data).reshape(ITEMS, K)
```

```python
import functools

import jax
import jax.numpy as jnp
from jax import lax
from jax.experimental import pallas as pl
from jax.experimental.pallas import tpu as pltpu
from jax.sharding import PartitionSpec as P

ITERS = 4
UNOBSERVED = 1024.0
PENALTY = 8.0
EPSILON = 1e-06
BIG_CHUNK = 32
SMALL_CHUNK = 8
VMEM_MIB = 60
GRID = 4
LOW, HIGH = (0, -1), (1, 2)
LONG_RING = (0, -1, 1, -2, 2, -3, 3, 4)
f32 = jnp.float32
bf16 = jnp.bfloat16


def split3(value):
    high = value.astype(bf16)
    rest = value - high.astype(f32)
    middle = rest.astype(bf16)
    low = (rest - middle.astype(f32)).astype(bf16)
    return jnp.concatenate([high, middle, low], axis=0)


def fold3(stacked):
    rows = stacked.shape[0] // 3
    return stacked[:rows] + (stacked[rows : 2 * rows] + stacked[2 * rows :])


def solve_kernel(
    place_ref, cols_ref, counts_ref, weights_ref, gram_ref, items_ref, *rest,
    groups, slots, blocks, tile, own, half
):
    sources = rest[: len(groups)]
    out_ref, tiles, flipped, confidence, *held_pieces, arrived = rest[len(groups) :]
    copies = [
        pltpu.make_async_copy(source, piece, arrived.at[index])
        for index, (source, piece) in enumerate(zip(sources, held_pieces))
    ]
    for copy in copies:
        copy.start()
    item_rows = blocks * own
    full = 2 * half
    small = SMALL_CHUNK * tile

    def each_live(visit, before=None):
        place = 0
        for index, (piece, (first_slot, held, members)) in enumerate(zip(held_pieces, groups)):
            if before is not None:
                before(index)
            for member, (down, right) in enumerate(members):
                sender = lax.rem(place_ref[0] + down + GRID, GRID) * GRID + lax.rem(
                    place_ref[1] + right + GRID, GRID
                )
                live = jnp.clip(counts_ref[sender] - first_slot, 0, held)

                def visit_slot(slot, carry, piece=piece, sender=sender, place=place, member=member):
                    visit(piece, member * held + slot, sender, first_slot + slot, place + slot)
                    return carry

                lax.fori_loop(0, live, visit_slot, 0)
                place = place + live
        return place

    total = lax.fori_loop(0, counts_ref.shape[0], lambda sender, sum: sum + counts_ref[sender], 0)
    padded = (total + SMALL_CHUNK - 1) // SMALL_CHUNK

    def clear(index, carry):
        at = pl.ds(pl.multiple_of(index * small, small), small)
        confidence[:, at] = jnp.zeros((item_rows, small), f32)
        return carry

    lax.fori_loop(0, padded, clear, 0)

    def clear_tail(place, carry):
        tiles[pl.ds(pl.multiple_of(place * tile, tile), tile), :] = jnp.zeros((tile, full), bf16)
        return carry

    lax.fori_loop(total, padded * SMALL_CHUNK, clear_tail, 0)

    def spread(piece, row, sender, slot, place):
        block = weights_ref[pl.ds(pl.multiple_of((sender * slots + slot) * own, own), own), :]
        target = pl.ds(pl.multiple_of(cols_ref[sender, slot] * own, own), own)
        confidence[target, pl.ds(pl.multiple_of(place * tile, tile), tile)] = block

    each_live(spread)

    def move(piece, row, sender, slot, place):
        block = piece[pl.ds(pl.multiple_of(row * tile, tile), tile), :]
        tiles[pl.ds(pl.multiple_of(place * tile, tile), tile), :] = block

    each_live(move, lambda index: copies[index].wait())

    def flip(index, carry):
        at = pl.ds(pl.multiple_of(index * small, small), small)
        flipped[:, at] = tiles[at, :].T
        return carry

    lax.fori_loop(0, padded, flip, 0)
    big_count = total // BIG_CHUNK
    small_first = big_count * (BIG_CHUNK // SMALL_CHUNK)

    gram = gram_ref[...]
    gram_high = gram.astype(bf16)
    gram_rest = gram - gram_high.astype(f32)
    gram_middle = gram_rest.astype(bf16)
    gram_low = (gram_rest - gram_middle.astype(f32)).astype(bf16)

    def gram_image(pieces, first, wide, out_first, out_wide):
        parts = [
            jnp.dot(
                pieces[: count * item_rows],
                part[first : first + wide, out_first : out_first + out_wide],
                preferred_element_type=f32,
            )
            for part, count in ((gram_high, 3), (gram_middle, 2), (gram_low, 1))
        ]
        high, middle, low = parts
        return jnp.concatenate(
            [
                high[:item_rows],
                high[item_rows : 2 * item_rows] + middle[:item_rows],
                high[2 * item_rows :] + middle[item_rows:] + low,
            ],
            axis=0,
        )

    def operate(vectors, first, wide, shift, out_first, out_wide):
        pieces = split3(vectors)

        def step(chunk, index, carry):
            at = pl.ds(pl.multiple_of(index * chunk, chunk), chunk)
            left = flipped[first : first + wide, at]
            inner = fold3(jnp.dot(pieces, left, preferred_element_type=f32))
            if shift:
                inner = inner - 1.0
            scaled = split3(confidence[:, at] * inner)
            right = tiles[at, out_first : out_first + out_wide]
            return carry + jnp.dot(scaled, right, preferred_element_type=f32)

        image = gram_image(pieces, first, wide, out_first, out_wide)
        image = lax.fori_loop(0, big_count, functools.partial(step, BIG_CHUNK * tile), image)
        image = lax.fori_loop(small_first, padded, functools.partial(step, small), image)
        return fold3(image)

    factors = items_ref[...]
    gradients = operate(factors, 0, full, True, 0, full) + PENALTY * factors
    later = gradients[:, half:]
    for block_index in range(2):
        first = block_index * half
        gradient = gradients[:, :half] if block_index == 0 else later
        residual = -gradient
        direction = residual
        norm_sq = jnp.sum(residual * residual, axis=1, keepdims=True)
        update = jnp.zeros_like(residual)
        for round_index in range(ITERS):
            width = full if block_index == 0 else half
            image = operate(direction, first, half, False, first, width)
            applied = image[:, :half] + PENALTY * direction
            step_size = norm_sq / (jnp.sum(direction * applied, axis=1, keepdims=True) + EPSILON)
            update = update + step_size * direction
            residual = residual - step_size * applied
            if block_index == 0:
                later = later + step_size * image[:, half:]
            if round_index + 1 < ITERS:
                norm_next = jnp.sum(residual * residual, axis=1, keepdims=True)
                direction = residual + (norm_next / (norm_sq + EPSILON)) * direction
                norm_sq = norm_next
        out_ref[:, first : first + half] = factors[:, first : first + half] + update


def solve(place, cols, counts, weights, gram, items, shipped, groups, *, tile, own):
    sources, slots = cols.shape
    item_rows, full = items.shape
    blocks = item_rows // own
    places = sources * slots
    kernel = functools.partial(
        solve_kernel, groups=groups, slots=slots, blocks=blocks, tile=tile, own=own, half=full // 2
    )
    smem = pl.BlockSpec(memory_space=pltpu.SMEM)
    vmem = pl.BlockSpec(memory_space=pltpu.VMEM)
    return pl.pallas_call(
        kernel,
        out_shape=jax.ShapeDtypeStruct((item_rows, full), f32),
        in_specs=[smem, smem, smem, vmem, vmem, vmem]
        + [pl.BlockSpec(memory_space=pl.ANY)] * len(shipped),
        out_specs=vmem,
        scratch_shapes=[
            pltpu.VMEM((places * tile, full), bf16),
            pltpu.VMEM((full, places * tile), bf16),
            pltpu.VMEM((item_rows, places * tile), f32),
            *[pltpu.VMEM(piece.shape, piece.dtype) for piece in shipped],
            pltpu.SemaphoreType.DMA((len(shipped),)),
        ],
        compiler_params=pltpu.CompilerParams(vmem_limit_bytes=VMEM_MIB * 1024 * 1024),
    )(place, cols, counts, weights, gram, items, *shipped)


def everywhere(value, axes):
    size = lax.axis_size(axes)
    return lax.all_to_all(
        jnp.broadcast_to(value[None], (size,) + value.shape), axes, 0, 0, tiled=True
    )


def send_x(value, step):
    pairs = [(y * GRID + x, y * GRID + (x + step) % GRID) for y in range(GRID) for x in range(GRID)]
    return lax.ppermute(value, "ub", pairs)


def send_y(value, step):
    pairs = [(y * GRID + x, (y + step) % GRID * GRID + x) for y in range(GRID) for x in range(GRID)]
    return lax.ppermute(value, "ub", pairs)


def send_z(value, step):
    size = lax.axis_size("ib") // 2
    pairs = [(z * 2 + c, (z + step) % size * 2 + c) for z in range(size) for c in range(2)]
    return lax.ppermute(value, "ib", pairs)


def send_core(value):
    size = lax.axis_size("ib")
    return lax.ppermute(value, "ib", [(i, i ^ 1) for i in range(size)])


def long_ring(value, beside):
    held = [value]
    below = above = value
    for _ in range(len(LONG_RING) // 2 - 1):
        below, above = send_z(below, 1), send_z(above, -1)
        held += [below, above]
    middle = value.shape[0] // 2
    below, above, beside = lax.optimization_barrier((below, above, beside))
    held += [send_z(below[:middle], 1), send_z(above[middle:], -1)]
    return jnp.concatenate(held, axis=0), beside


def pick_kernel(order_ref, near_ref, other_ref, x_ref, y_ref, gram_ref, *, tile, half):
    places = near_ref.shape[0] // tile

    def pick(slot, target, first):
        at = pl.ds(pl.multiple_of((slot - first) * tile, tile), tile)
        row = order_ref[slot]

        @pl.when(row < places)
        def _():
            target[at, :] = near_ref[pl.ds(pl.multiple_of(row * tile, tile), tile), :]

        @pl.when(row >= places)
        def _():
            target[at, :] = other_ref[pl.ds(pl.multiple_of((row - places) * tile, tile), tile), :]

    each = x_ref.shape[0] // tile
    for target, first in ((x_ref, 0), (y_ref, each)):

        def step(slot, carry, target=target, first=first):
            pick(slot, target, first)
            return carry

        lax.fori_loop(first, first + each, step, 0)
    for index, (left, right) in enumerate(((0, 0), (0, half), (half, half))):
        gram_ref[index * half : (index + 1) * half, :] = sum(
            lax.dot_general(
                users[:, left : left + half],
                users[:, right : right + half],
                (((0,), (0,)), ((), ())),
                preferred_element_type=f32,
            )
            for users in (near_ref, other_ref)
        )


def pick_tiles(order, near, other, *, tile):
    full = near.shape[1]
    half = full // 2
    each = order.shape[0] // 2
    vmem = pl.BlockSpec(memory_space=pltpu.VMEM)
    return pl.pallas_call(
        functools.partial(pick_kernel, tile=tile, half=half),
        out_shape=[
            jax.ShapeDtypeStruct((each * tile, full), bf16),
            jax.ShapeDtypeStruct((each * tile, full), bf16),
            jax.ShapeDtypeStruct((3 * half, half), f32),
        ],
        in_specs=[pl.BlockSpec(memory_space=pltpu.SMEM), vmem, vmem],
        out_specs=[vmem, vmem, vmem],
        compiler_params=pltpu.CompilerParams(vmem_limit_bytes=16 * 1024 * 1024),
    )(order, near, other)


def plan(slots):
    half = slots // 2
    groups = []
    for turn in range(2):
        for outer, inner in ((0, LOW), (0, HIGH), (-1, LOW), (1, HIGH), (1, LOW), (-1, HIGH), (2, LOW), (2, HIGH)):
            members = [(outer, i) if turn == 0 else (i, outer) for i in inner]
            groups.append((turn * half, half, members))
    return groups


def copy_kernel(*refs, parts):
    sources, targets = refs[: -len(parts)], refs[-len(parts) :]
    for target, pieces in zip(targets, parts):
        at = 0
        for index, first, rows in pieces:
            target[at : at + rows, :] = sources[index][first : first + rows, :]
            at += rows


def rearrange(sources, parts):
    vmem = pl.BlockSpec(memory_space=pltpu.VMEM)
    return pl.pallas_call(
        functools.partial(copy_kernel, parts=parts),
        out_shape=[
            jax.ShapeDtypeStruct((sum(rows for _, _, rows in pieces), sources[0].shape[1]), bf16)
            for pieces in parts
        ],
        in_specs=[vmem] * len(sources),
        out_specs=[vmem] * len(parts),
        compiler_params=pltpu.CompilerParams(vmem_limit_bytes=20 * 1024 * 1024),
    )(*sources)


def ship(along_x, along_y, blocks):
    rows = along_x.shape[0]
    near = []
    for value, send in ((along_x, send_x), (along_y, send_y)):
        near += [value, send(value, 1), send(value, -1)]
    far = []
    for (below, above), send in ((near[1:3], send_x), (near[4:6], send_y)):
        far += [send(below[: rows // 2], 1), send(above[rows // 2 :], -1)]
    near, far, blocks = lax.optimization_barrier((near, far, blocks))
    lows_and_highs = rearrange(
        near + far,
        [
            pieces
            for turn in range(2)
            for pieces in (
                [(3 * turn, 0, rows), (3 * turn + 1, 0, rows)],
                [(3 * turn + 2, 0, rows)] + [(6 + 2 * turn + i, 0, rows // 2) for i in range(2)],
            )
        ],
    )
    sends = (send_y, send_y, send_x, send_x)
    steps = (1, -1, 1, -1)
    ub = lax.axis_size("ub")
    first = [send(value, step) for send, value, step in zip(sends, lows_and_highs, steps)]
    part = lax.all_to_all(blocks.reshape(ub, -1, blocks.shape[1]), "ub", 0, 0, tiled=True)
    first, lows_and_highs, part = lax.optimization_barrier((first, lows_and_highs, part))
    opposite = [send(value, step) for send, value, step in zip(sends, first, steps)]
    summed = everywhere(jnp.sum(part, axis=0), "ub").reshape(blocks.shape)
    opposite, lows_and_highs, summed = lax.optimization_barrier((opposite, lows_and_highs, summed))
    second = [send(value, -step) for send, value, step in zip(sends, lows_and_highs, steps)]
    shipped = []
    for turn in (slice(0, 2), slice(2, 4)):
        shipped += [*lows_and_highs[turn], *first[turn], *second[turn], *opposite[turn]]
    return shipped, summed


def per_device(user_factors, item_factors, tile_rows, tile_cols, tile_count, tile_weights):
    ub = lax.axis_size("ub")
    ib = lax.axis_size("ib")
    tile = tile_weights.shape[-1]
    slots = tile_rows.shape[-1]
    shard, full = user_factors.shape
    items = item_factors.shape[0]
    blocks = items // tile
    own = tile // ub
    user_total = shard * ub * ib
    me = lax.axis_index("ub")

    meta = jnp.concatenate(
        [tile_cols.reshape(-1), tile_count.reshape(1), jnp.zeros((tile - slots - 1,), jnp.int32)]
    ).astype(bf16)
    mine = tile_weights.reshape(slots, tile, ub, own).transpose(2, 0, 3, 1)
    mine = mine.reshape(ub, slots * own, tile)
    mine = jnp.concatenate([mine, jnp.broadcast_to(meta, (ub, 16, tile))], axis=1)
    got = lax.all_to_all(mine, "ub", 0, 0, tiled=True)

    held = shard // tile
    my_ib = lax.axis_index("ib")
    same_core, got = long_ring(user_factors.reshape(held, tile, full), got)
    wanted = tile_rows.reshape(slots)
    at_z, at_core = wanted // held // 2, wanted // held % 2
    spot = [0] * len(LONG_RING)
    for index, offset in enumerate(LONG_RING):
        spot[offset % len(LONG_RING)] = index
    order = jnp.array(spot, jnp.int32)[(at_z - my_ib // 2) % len(LONG_RING)]
    order = order + len(LONG_RING) * (at_core != my_ib % 2)
    near = same_core.reshape(-1, full)
    along_x, along_y, local = pick_tiles(
        order * held + wanted % held, near, send_core(near), tile=tile
    )
    shipped, local = ship(along_x, along_y, local)
    half = full // 2
    local = local * (UNOBSERVED / user_total)
    corner, across, last = jnp.split(local, 3, axis=0)
    gram = jnp.block([[corner, across], [across.T, last]])
    weights = got[:, : slots * own].reshape(ub * slots * own, tile).astype(f32)
    cols = got[:, slots * own, :slots].astype(jnp.int32)
    counts = got[:, slots * own, slots].astype(jnp.int32)

    own_items = lax.dynamic_slice_in_dim(
        item_factors.reshape(blocks, ub, own, full), me, 1, axis=1
    ).reshape(blocks * own, full)
    place = jnp.stack([me // GRID, me % GRID])
    result = solve(
        place, cols, counts, weights, gram, own_items, shipped, plan(slots), tile=tile, own=own
    )
    result = everywhere(result, "ub").reshape(ub, blocks, own, full)
    return result.transpose(1, 0, 2, 3).reshape(items, full)


def solution(mesh):
    in_specs = (
        P(("ub", "ib"), None),
        P("ib", None),
        P("ub", "ib", None),
        P("ub", "ib", None),
        P("ub", "ib"),
        P("ub", "ib", None, None, None),
    )
    return jax.shard_map(
        per_device, mesh=mesh, in_specs=in_specs, out_specs=P("ib", None), check_vma=False
    )
```

```python
import functools

import jax
import jax.numpy as jnp
from jax import lax
from jax.experimental import pallas as pl
from jax.experimental.pallas import tpu as pltpu
from jax.sharding import PartitionSpec as P

ITERS = 4
UNOBSERVED = 1024.0
PENALTY = 8.0
EPSILON = 1e-06
CHUNKS = (48, 16, 8)
SMALL_CHUNK = CHUNKS[-1]
VMEM_MIB = 60
GRID = 4
LOW, HIGH = (0, -1), (1, 2)
LONG_RING = (0, -1, 1, -2, 2, -3, 3, 4)
f32 = jnp.float32
bf16 = jnp.bfloat16


def split3(value):
    high = value.astype(bf16)
    rest = value - high.astype(f32)
    middle = rest.astype(bf16)
    low = (rest - middle.astype(f32)).astype(bf16)
    return jnp.concatenate([high, middle, low], axis=0)


def fold3(stacked):
    rows = stacked.shape[0] // 3
    return stacked[:rows] + (stacked[rows : 2 * rows] + stacked[2 * rows :])


def solve_kernel(
    place_ref, cols_ref, counts_ref, weights_ref, gram_ref, items_ref, *rest,
    groups, slots, blocks, tile, own, half
):
    shipped = rest[: len(groups)]
    out_ref, tiles, flipped, confidence, copies = rest[len(groups) :]
    item_rows = blocks * own
    full = 2 * half
    small = SMALL_CHUNK * tile

    def tile_copy(source, row, place):
        return pltpu.make_async_copy(
            source.at[pl.ds(pl.multiple_of(row * tile, tile), tile), :],
            tiles.at[pl.ds(pl.multiple_of(place * tile, tile), tile), :],
            copies,
        )

    def each_live(visit):
        place = 0
        for piece, (first_slot, held, members) in zip(shipped, groups):
            for member, (down, right) in enumerate(members):
                sender = lax.rem(place_ref[0] + down + GRID, GRID) * GRID + lax.rem(
                    place_ref[1] + right + GRID, GRID
                )
                live = jnp.clip(counts_ref[sender] - first_slot, 0, held)

                def visit_slot(slot, carry, piece=piece, sender=sender, place=place, member=member):
                    visit(piece, member * held + slot, sender, first_slot + slot, place + slot)
                    return carry

                lax.fori_loop(0, live, visit_slot, 0)
                place = place + live
        return place

    total = each_live(lambda piece, row, sender, slot, place: tile_copy(piece, row, place).start())
    padded = (total + SMALL_CHUNK - 1) // SMALL_CHUNK

    def clear(index, carry):
        at = pl.ds(pl.multiple_of(index * small, small), small)
        confidence[:, at] = jnp.zeros((item_rows, small), f32)
        return carry

    lax.fori_loop(0, padded, clear, 0)

    def clear_tail(place, carry):
        tiles[pl.ds(pl.multiple_of(place * tile, tile), tile), :] = jnp.zeros((tile, full), bf16)
        return carry

    lax.fori_loop(total, padded * SMALL_CHUNK, clear_tail, 0)

    def spread(piece, row, sender, slot, place):
        block = weights_ref[pl.ds(pl.multiple_of((sender * slots + slot) * own, own), own), :]
        target = pl.ds(pl.multiple_of(cols_ref[sender, slot] * own, own), own)
        confidence[target, pl.ds(pl.multiple_of(place * tile, tile), tile)] = block

    each_live(spread)

    def wait_slot(place, carry):
        tile_copy(shipped[0], 0, place).wait()
        return carry

    lax.fori_loop(0, total, wait_slot, 0)

    def flip(index, carry):
        at = pl.ds(pl.multiple_of(index * small, small), small)
        flipped[:, at] = tiles[at, :].T
        return carry

    lax.fori_loop(0, padded, flip, 0)
    spans = []
    done = 0
    for size in CHUNKS:
        count = (padded * SMALL_CHUNK - done) // size
        spans.append((size * tile, done * tile, count))
        done = done + count * size

    gram = gram_ref[...]
    gram_high = gram.astype(bf16)
    gram_rest = gram - gram_high.astype(f32)
    gram_middle = gram_rest.astype(bf16)
    gram_low = (gram_rest - gram_middle.astype(f32)).astype(bf16)

    def gram_image(pieces, first, wide, out_first, out_wide):
        parts = [
            jnp.dot(
                pieces[: count * item_rows],
                part[first : first + wide, out_first : out_first + out_wide],
                preferred_element_type=f32,
            )
            for part, count in ((gram_high, 3), (gram_middle, 2), (gram_low, 1))
        ]
        high, middle, low = parts
        return jnp.concatenate(
            [
                high[:item_rows],
                high[item_rows : 2 * item_rows] + middle[:item_rows],
                high[2 * item_rows :] + middle[item_rows:] + low,
            ],
            axis=0,
        )

    def operate(vectors, first, wide, shift, out_first, out_wide):
        pieces = split3(vectors)

        def step(chunk, start, index, carry):
            at = pl.ds(pl.multiple_of(start + index * chunk, small), chunk)
            left = flipped[first : first + wide, at]
            inner = fold3(jnp.dot(pieces, left, preferred_element_type=f32))
            if shift:
                inner = inner - 1.0
            scaled = split3(confidence[:, at] * inner)
            right = tiles[at, out_first : out_first + out_wide]
            return carry + jnp.dot(scaled, right, preferred_element_type=f32)

        image = gram_image(pieces, first, wide, out_first, out_wide)
        for chunk, start, count in spans:
            image = lax.fori_loop(0, count, functools.partial(step, chunk, start), image)
        return fold3(image)

    factors = items_ref[...]
    gradients = operate(factors, 0, full, True, 0, full) + PENALTY * factors
    later = gradients[:, half:]
    for block_index in range(2):
        first = block_index * half
        gradient = gradients[:, :half] if block_index == 0 else later
        residual = -gradient
        direction = residual
        norm_sq = jnp.sum(residual * residual, axis=1, keepdims=True)
        update = jnp.zeros_like(residual)
        for round_index in range(ITERS):
            width = full if block_index == 0 else half
            image = operate(direction, first, half, False, first, width)
            applied = image[:, :half] + PENALTY * direction
            step_size = norm_sq / (jnp.sum(direction * applied, axis=1, keepdims=True) + EPSILON)
            update = update + step_size * direction
            residual = residual - step_size * applied
            if block_index == 0:
                later = later + step_size * image[:, half:]
            if round_index + 1 < ITERS:
                norm_next = jnp.sum(residual * residual, axis=1, keepdims=True)
                direction = residual + (norm_next / (norm_sq + EPSILON)) * direction
                norm_sq = norm_next
        solved = factors[:, first : first + half] + update
        out_ref[:, :, first : first + half] = jnp.broadcast_to(solved[None], (out_ref.shape[0],) + solved.shape)


def solve(place, cols, counts, weights, gram, items, shipped, groups, *, tile, own):
    sources, slots = cols.shape
    item_rows, full = items.shape
    blocks = item_rows // own
    places = sources * slots
    kernel = functools.partial(
        solve_kernel, groups=groups, slots=slots, blocks=blocks, tile=tile, own=own, half=full // 2
    )
    smem = pl.BlockSpec(memory_space=pltpu.SMEM)
    vmem = pl.BlockSpec(memory_space=pltpu.VMEM)
    return pl.pallas_call(
        kernel,
        out_shape=jax.ShapeDtypeStruct((sources, item_rows, full), f32),
        in_specs=[smem, smem, smem, vmem, vmem, vmem]
        + [pl.BlockSpec(memory_space=pl.ANY)] * len(shipped),
        out_specs=vmem,
        scratch_shapes=[
            pltpu.VMEM((places * tile, full), bf16),
            pltpu.VMEM((full, places * tile), bf16),
            pltpu.VMEM((item_rows, places * tile), f32),
            pltpu.SemaphoreType.DMA,
        ],
        compiler_params=pltpu.CompilerParams(vmem_limit_bytes=VMEM_MIB * 1024 * 1024),
    )(place, cols, counts, weights, gram, items, *shipped)


def everywhere(value, axes):
    size = lax.axis_size(axes)
    return lax.all_to_all(
        jnp.broadcast_to(value[None], (size,) + value.shape), axes, 0, 0, tiled=True
    )


def send_x(value, step):
    pairs = [(y * GRID + x, y * GRID + (x + step) % GRID) for y in range(GRID) for x in range(GRID)]
    return lax.ppermute(value, "ub", pairs)


def send_y(value, step):
    pairs = [(y * GRID + x, (y + step) % GRID * GRID + x) for y in range(GRID) for x in range(GRID)]
    return lax.ppermute(value, "ub", pairs)


def send_z(value, step):
    size = lax.axis_size("ib") // 2
    pairs = [(z * 2 + c, (z + step) % size * 2 + c) for z in range(size) for c in range(2)]
    return lax.ppermute(value, "ib", pairs)


def send_core(value):
    size = lax.axis_size("ib")
    return lax.ppermute(value, "ib", [(i, i ^ 1) for i in range(size)])


def long_ring(value, beside):
    held = [value]
    below = above = value
    for _ in range(len(LONG_RING) // 2 - 1):
        below, above = send_z(below, 1), send_z(above, -1)
        held += [below, above]
    middle = value.shape[0] // 2
    below, above, beside = lax.optimization_barrier((below, above, beside))
    held += [send_z(below[:middle], 1), send_z(above[middle:], -1)]
    return jnp.concatenate(held, axis=0), beside


def pick_kernel(order_ref, near_ref, other_ref, x_ref, y_ref, gram_ref, *, tile, half):
    places = near_ref.shape[0] // tile

    def pick(slot, target, first):
        at = pl.ds(pl.multiple_of((slot - first) * tile, tile), tile)
        row = order_ref[slot]

        @pl.when(row < places)
        def _():
            target[at, :] = near_ref[pl.ds(pl.multiple_of(row * tile, tile), tile), :]

        @pl.when(row >= places)
        def _():
            target[at, :] = other_ref[pl.ds(pl.multiple_of((row - places) * tile, tile), tile), :]

    each = x_ref.shape[0] // tile
    for target, first in ((x_ref, 0), (y_ref, each)):

        def step(slot, carry, target=target, first=first):
            pick(slot, target, first)
            return carry

        lax.fori_loop(first, first + each, step, 0)
    for index, (left, right) in enumerate(((0, 0), (0, half), (half, half))):
        gram_ref[index * half : (index + 1) * half, :] = sum(
            lax.dot_general(
                users[:, left : left + half],
                users[:, right : right + half],
                (((0,), (0,)), ((), ())),
                preferred_element_type=f32,
            )
            for users in (near_ref, other_ref)
        )


def pick_tiles(order, near, other, *, tile):
    full = near.shape[1]
    half = full // 2
    each = order.shape[0] // 2
    vmem = pl.BlockSpec(memory_space=pltpu.VMEM)
    return pl.pallas_call(
        functools.partial(pick_kernel, tile=tile, half=half),
        out_shape=[
            jax.ShapeDtypeStruct((each * tile, full), bf16),
            jax.ShapeDtypeStruct((each * tile, full), bf16),
            jax.ShapeDtypeStruct((3 * half, half), f32),
        ],
        in_specs=[pl.BlockSpec(memory_space=pltpu.SMEM), vmem, vmem],
        out_specs=[vmem, vmem, vmem],
        compiler_params=pltpu.CompilerParams(vmem_limit_bytes=16 * 1024 * 1024),
    )(order, near, other)


def plan(slots):
    half = slots // 2
    groups = []
    for turn in range(2):
        for outer, inner in ((0, LOW), (0, HIGH), (-1, LOW), (1, HIGH), (1, LOW), (-1, HIGH), (2, LOW), (2, HIGH)):
            members = [(outer, i) if turn == 0 else (i, outer) for i in inner]
            groups.append((turn * half, half, members))
    return groups


def copy_kernel(*refs, parts):
    sources, targets = refs[: -len(parts)], refs[-len(parts) :]
    for target, pieces in zip(targets, parts):
        at = 0
        for index, first, rows in pieces:
            target[at : at + rows, :] = sources[index][first : first + rows, :]
            at += rows


def rearrange(sources, parts):
    vmem = pl.BlockSpec(memory_space=pltpu.VMEM)
    return pl.pallas_call(
        functools.partial(copy_kernel, parts=parts),
        out_shape=[
            jax.ShapeDtypeStruct((sum(rows for _, _, rows in pieces), sources[0].shape[1]), bf16)
            for pieces in parts
        ],
        in_specs=[vmem] * len(sources),
        out_specs=[vmem] * len(parts),
        compiler_params=pltpu.CompilerParams(vmem_limit_bytes=20 * 1024 * 1024),
    )(*sources)


def ship(along_x, along_y, blocks):
    rows = along_x.shape[0]
    near = []
    for value, send in ((along_x, send_x), (along_y, send_y)):
        near += [value, send(value, 1), send(value, -1)]
    far = []
    for (below, above), send in ((near[1:3], send_x), (near[4:6], send_y)):
        far += [send(below[: rows // 2], 1), send(above[rows // 2 :], -1)]
    near, far, blocks = lax.optimization_barrier((near, far, blocks))
    lows_and_highs = rearrange(
        near + far,
        [
            pieces
            for turn in range(2)
            for pieces in (
                [(3 * turn, 0, rows), (3 * turn + 1, 0, rows)],
                [(3 * turn + 2, 0, rows)] + [(6 + 2 * turn + i, 0, rows // 2) for i in range(2)],
            )
        ],
    )
    sends = (send_y, send_y, send_x, send_x)
    steps = (1, -1, 1, -1)
    ub = lax.axis_size("ub")
    first = [send(value, step) for send, value, step in zip(sends, lows_and_highs, steps)]
    part = lax.all_to_all(blocks.reshape(ub, -1, blocks.shape[1]), "ub", 0, 0, tiled=True)
    first, lows_and_highs, part = lax.optimization_barrier((first, lows_and_highs, part))
    opposite = [send(value, step) for send, value, step in zip(sends, first, steps)]
    summed = everywhere(jnp.sum(part, axis=0), "ub").reshape(blocks.shape)
    opposite, lows_and_highs, summed = lax.optimization_barrier((opposite, lows_and_highs, summed))
    second = [send(value, -step) for send, value, step in zip(sends, lows_and_highs, steps)]
    shipped = []
    for turn in (slice(0, 2), slice(2, 4)):
        shipped += [*lows_and_highs[turn], *first[turn], *second[turn], *opposite[turn]]
    return shipped, summed


def per_device(user_factors, item_factors, tile_rows, tile_cols, tile_count, tile_weights):
    ub = lax.axis_size("ub")
    ib = lax.axis_size("ib")
    tile = tile_weights.shape[-1]
    slots = tile_rows.shape[-1]
    shard, full = user_factors.shape
    items = item_factors.shape[0]
    blocks = items // tile
    own = tile // ub
    user_total = shard * ub * ib
    me = lax.axis_index("ub")

    meta = jnp.concatenate(
        [tile_cols.reshape(-1), tile_count.reshape(1), jnp.zeros((tile - slots - 1,), jnp.int32)]
    ).astype(bf16)
    mine = tile_weights.reshape(slots, tile, ub, own).transpose(2, 0, 3, 1)
    mine = mine.reshape(ub, slots * own, tile)
    mine = jnp.concatenate([mine, jnp.broadcast_to(meta, (ub, 16, tile))], axis=1)
    got = lax.all_to_all(mine, "ub", 0, 0, tiled=True)

    held = shard // tile
    my_ib = lax.axis_index("ib")
    same_core, got = long_ring(user_factors.reshape(held, tile, full), got)
    wanted = tile_rows.reshape(slots)
    at_z, at_core = wanted // held // 2, wanted // held % 2
    spot = [0] * len(LONG_RING)
    for index, offset in enumerate(LONG_RING):
        spot[offset % len(LONG_RING)] = index
    order = jnp.array(spot, jnp.int32)[(at_z - my_ib // 2) % len(LONG_RING)]
    order = order + len(LONG_RING) * (at_core != my_ib % 2)
    near = same_core.reshape(-1, full)
    along_x, along_y, local = pick_tiles(
        order * held + wanted % held, near, send_core(near), tile=tile
    )
    shipped, local = ship(along_x, along_y, local)
    half = full // 2
    local = local * (UNOBSERVED / user_total)
    corner, across, last = jnp.split(local, 3, axis=0)
    gram = jnp.block([[corner, across], [across.T, last]])
    weights = got[:, : slots * own].reshape(ub * slots * own, tile).astype(f32)
    cols = got[:, slots * own, :slots].astype(jnp.int32)
    counts = got[:, slots * own, slots].astype(jnp.int32)

    own_items = lax.dynamic_slice_in_dim(
        item_factors.reshape(blocks, ub, own, full), me, 1, axis=1
    ).reshape(blocks * own, full)
    place = jnp.stack([me // GRID, me % GRID])
    result = solve(
        place, cols, counts, weights, gram, own_items, shipped, plan(slots), tile=tile, own=own
    )
    result = lax.all_to_all(result, "ub", 0, 0, tiled=True).reshape(ub, blocks, own, full)
    return result.transpose(1, 0, 2, 3).reshape(items, full)


def solution(mesh):
    in_specs = (
        P(("ub", "ib"), None),
        P("ib", None),
        P("ub", "ib", None),
        P("ub", "ib", None),
        P("ub", "ib"),
        P("ub", "ib", None, None, None),
    )
    return jax.shard_map(
        per_device, mesh=mesh, in_specs=in_specs, out_specs=P("ib", None), check_vma=False
    )
```

```python
import functools

import jax
import jax.numpy as jnp
from jax import lax
from jax.experimental import pallas as pl
from jax.experimental.pallas import tpu as pltpu
from jax.sharding import PartitionSpec as P

ITERS = 4
UNOBSERVED = 1024.0
PENALTY = 8.0
EPSILON = 1e-06
CHUNKS = (32, 8)
SMALL_CHUNK = CHUNKS[-1]
VMEM_MIB = 60
GRID = 4
LOW, HIGH = (0, -1), (1, 2)
LONG_RING = (0, -1, 1, -2, 2, -3, 3, 4)
f32 = jnp.float32
bf16 = jnp.bfloat16


def split3(value):
    high = value.astype(bf16)
    rest = value - high.astype(f32)
    middle = rest.astype(bf16)
    low = (rest - middle.astype(f32)).astype(bf16)
    return jnp.concatenate([high, middle, low], axis=0)


def fold3(stacked):
    rows = stacked.shape[0] // 3
    return stacked[:rows] + (stacked[rows : 2 * rows] + stacked[2 * rows :])


def solve_kernel(
    place_ref, cols_ref, counts_ref, weights_ref, gram_ref, items_ref, *rest,
    groups, slots, blocks, tile, own, half
):
    shipped = rest[: len(groups)]
    out_ref, tiles, flipped, confidence, copies = rest[len(groups) :]
    item_rows = blocks * own
    full = 2 * half
    small = SMALL_CHUNK * tile

    def tile_copy(source, row, place):
        return pltpu.make_async_copy(
            source.at[pl.ds(pl.multiple_of(row * tile, tile), tile), :],
            tiles.at[pl.ds(pl.multiple_of(place * tile, tile), tile), :],
            copies,
        )

    def each_live(visit):
        place = 0
        for piece, (first_slot, held, members) in zip(shipped, groups):
            for member, (down, right) in enumerate(members):
                sender = lax.rem(place_ref[0] + down + GRID, GRID) * GRID + lax.rem(
                    place_ref[1] + right + GRID, GRID
                )
                live = jnp.clip(counts_ref[sender] - first_slot, 0, held)

                def visit_slot(slot, carry, piece=piece, sender=sender, place=place, member=member):
                    visit(piece, member * held + slot, sender, first_slot + slot, place + slot)
                    return carry

                lax.fori_loop(0, live, visit_slot, 0)
                place = place + live
        return place

    total = each_live(lambda piece, row, sender, slot, place: tile_copy(piece, row, place).start())
    padded = (total + SMALL_CHUNK - 1) // SMALL_CHUNK

    def clear(index, carry):
        at = pl.ds(pl.multiple_of(index * small, small), small)
        confidence[:, at] = jnp.zeros((item_rows, small), f32)
        return carry

    lax.fori_loop(0, padded, clear, 0)

    def clear_tail(place, carry):
        tiles[pl.ds(pl.multiple_of(place * tile, tile), tile), :] = jnp.zeros((tile, full), bf16)
        return carry

    lax.fori_loop(total, padded * SMALL_CHUNK, clear_tail, 0)

    def spread(piece, row, sender, slot, place):
        block = weights_ref[pl.ds(pl.multiple_of((sender * slots + slot) * own, own), own), :]
        target = pl.ds(pl.multiple_of(cols_ref[sender, slot] * own, own), own)
        confidence[target, pl.ds(pl.multiple_of(place * tile, tile), tile)] = block

    each_live(spread)

    def wait_slot(place, carry):
        tile_copy(shipped[0], 0, place).wait()
        return carry

    lax.fori_loop(0, total, wait_slot, 0)

    def flip(index, carry):
        at = pl.ds(pl.multiple_of(index * small, small), small)
        flipped[:, at] = tiles[at, :].T
        return carry

    lax.fori_loop(0, padded, flip, 0)
    spans = []
    done = 0
    for size in CHUNKS:
        count = (padded * SMALL_CHUNK - done) // size
        spans.append((size * tile, done * tile, count))
        done = done + count * size

    gram = gram_ref[...]
    gram_high = gram.astype(bf16)
    gram_rest = gram - gram_high.astype(f32)
    gram_middle = gram_rest.astype(bf16)
    gram_low = (gram_rest - gram_middle.astype(f32)).astype(bf16)

    def gram_image(pieces, first, wide, out_first, out_wide):
        parts = [
            jnp.dot(
                pieces[: count * item_rows],
                part[first : first + wide, out_first : out_first + out_wide],
                preferred_element_type=f32,
            )
            for part, count in ((gram_high, 3), (gram_middle, 2), (gram_low, 1))
        ]
        high, middle, low = parts
        return jnp.concatenate(
            [
                high[:item_rows],
                high[item_rows : 2 * item_rows] + middle[:item_rows],
                high[2 * item_rows :] + middle[item_rows:] + low,
            ],
            axis=0,
        )

    def operate(vectors, first, wide, shift, out_first, out_wide):
        pieces = split3(vectors)

        def step(chunk, start, index, carry):
            at = pl.ds(pl.multiple_of(start + index * chunk, small), chunk)
            left = flipped[first : first + wide, at]
            inner = fold3(jnp.dot(pieces, left, preferred_element_type=f32))
            if shift:
                inner = inner - 1.0
            scaled = split3(confidence[:, at] * inner)
            right = tiles[at, out_first : out_first + out_wide]
            return carry + jnp.dot(scaled, right, preferred_element_type=f32)

        image = gram_image(pieces, first, wide, out_first, out_wide)
        for chunk, start, count in spans:
            image = lax.fori_loop(0, count, functools.partial(step, chunk, start), image)
        return fold3(image)

    factors = items_ref[...]
    gradients = operate(factors, 0, full, True, 0, full) + PENALTY * factors
    later = gradients[:, half:]
    for block_index in range(2):
        first = block_index * half
        gradient = gradients[:, :half] if block_index == 0 else later
        residual = -gradient
        direction = residual
        norm_sq = jnp.sum(residual * residual, axis=1, keepdims=True)
        update = jnp.zeros_like(residual)
        for round_index in range(ITERS):
            width = full if block_index == 0 else half
            image = operate(direction, first, half, False, first, width)
            applied = image[:, :half] + PENALTY * direction
            step_size = norm_sq / (jnp.sum(direction * applied, axis=1, keepdims=True) + EPSILON)
            update = update + step_size * direction
            residual = residual - step_size * applied
            if block_index == 0:
                later = later + step_size * image[:, half:]
            if round_index + 1 < ITERS:
                norm_next = jnp.sum(residual * residual, axis=1, keepdims=True)
                direction = residual + (norm_next / (norm_sq + EPSILON)) * direction
                norm_sq = norm_next
        solved = factors[:, first : first + half] + update
        out_ref[:, first : first + half] = solved


def solve(place, cols, counts, weights, gram, items, shipped, groups, *, tile, own):
    sources, slots = cols.shape
    item_rows, full = items.shape
    blocks = item_rows // own
    places = sources * slots
    kernel = functools.partial(
        solve_kernel, groups=groups, slots=slots, blocks=blocks, tile=tile, own=own, half=full // 2
    )
    smem = pl.BlockSpec(memory_space=pltpu.SMEM)
    vmem = pl.BlockSpec(memory_space=pltpu.VMEM)
    return pl.pallas_call(
        kernel,
        out_shape=jax.ShapeDtypeStruct((item_rows, full), f32),
        in_specs=[smem, smem, smem, vmem, vmem, vmem]
        + [pl.BlockSpec(memory_space=pl.ANY)] * len(shipped),
        out_specs=vmem,
        scratch_shapes=[
            pltpu.VMEM((places * tile, full), bf16),
            pltpu.VMEM((full, places * tile), bf16),
            pltpu.VMEM((item_rows, places * tile), f32),
            pltpu.SemaphoreType.DMA,
        ],
        compiler_params=pltpu.CompilerParams(vmem_limit_bytes=VMEM_MIB * 1024 * 1024),
    )(place, cols, counts, weights, gram, items, *shipped)


def everywhere(value, axes):
    size = lax.axis_size(axes)
    return lax.all_to_all(
        jnp.broadcast_to(value[None], (size,) + value.shape), axes, 0, 0, tiled=True
    )


def send_x(value, step):
    pairs = [(y * GRID + x, y * GRID + (x + step) % GRID) for y in range(GRID) for x in range(GRID)]
    return lax.ppermute(value, "ub", pairs)


def send_y(value, step):
    pairs = [(y * GRID + x, (y + step) % GRID * GRID + x) for y in range(GRID) for x in range(GRID)]
    return lax.ppermute(value, "ub", pairs)


def send_z(value, step):
    size = lax.axis_size("ib") // 2
    pairs = [(z * 2 + c, (z + step) % size * 2 + c) for z in range(size) for c in range(2)]
    return lax.ppermute(value, "ib", pairs)


def send_core(value):
    size = lax.axis_size("ib")
    return lax.ppermute(value, "ib", [(i, i ^ 1) for i in range(size)])


def long_ring(value, beside):
    held = [value]
    below = above = value
    for _ in range(len(LONG_RING) // 2 - 1):
        below, above = send_z(below, 1), send_z(above, -1)
        held += [below, above]
    middle = value.shape[0] // 2
    below, above, beside = lax.optimization_barrier((below, above, beside))
    held += [send_z(below[:middle], 1), send_z(above[middle:], -1)]
    return jnp.concatenate(held, axis=0), beside


def pick_kernel(order_ref, near_ref, other_ref, x_ref, y_ref, gram_ref, *, tile, half):
    places = near_ref.shape[0] // tile

    def pick(slot, target, first):
        at = pl.ds(pl.multiple_of((slot - first) * tile, tile), tile)
        row = order_ref[slot]

        @pl.when(row < places)
        def _():
            target[at, :] = near_ref[pl.ds(pl.multiple_of(row * tile, tile), tile), :]

        @pl.when(row >= places)
        def _():
            target[at, :] = other_ref[pl.ds(pl.multiple_of((row - places) * tile, tile), tile), :]

    each = x_ref.shape[0] // tile
    for target, first in ((x_ref, 0), (y_ref, each)):

        def step(slot, carry, target=target, first=first):
            pick(slot, target, first)
            return carry

        lax.fori_loop(first, first + each, step, 0)
    for index, (left, right) in enumerate(((0, 0), (0, half), (half, half))):
        gram_ref[index * half : (index + 1) * half, :] = sum(
            lax.dot_general(
                users[:, left : left + half],
                users[:, right : right + half],
                (((0,), (0,)), ((), ())),
                preferred_element_type=f32,
            )
            for users in (near_ref, other_ref)
        )


def pick_tiles(order, near, other, *, tile):
    full = near.shape[1]
    half = full // 2
    each = order.shape[0] // 2
    vmem = pl.BlockSpec(memory_space=pltpu.VMEM)
    return pl.pallas_call(
        functools.partial(pick_kernel, tile=tile, half=half),
        out_shape=[
            jax.ShapeDtypeStruct((each * tile, full), bf16),
            jax.ShapeDtypeStruct((each * tile, full), bf16),
            jax.ShapeDtypeStruct((3 * half, half), f32),
        ],
        in_specs=[pl.BlockSpec(memory_space=pltpu.SMEM), vmem, vmem],
        out_specs=[vmem, vmem, vmem],
        compiler_params=pltpu.CompilerParams(vmem_limit_bytes=16 * 1024 * 1024),
    )(order, near, other)


def plan(slots):
    half = slots // 2
    groups = []
    for turn in range(2):
        for outer, inner in ((0, LOW), (0, HIGH), (-1, LOW), (1, HIGH), (1, LOW), (-1, HIGH), (2, LOW), (2, HIGH)):
            members = [(outer, i) if turn == 0 else (i, outer) for i in inner]
            groups.append((turn * half, half, members))
    return groups


def copy_kernel(*refs, parts):
    sources, targets = refs[: -len(parts)], refs[-len(parts) :]
    for target, pieces in zip(targets, parts):
        at = 0
        for index, first, rows in pieces:
            target[at : at + rows, :] = sources[index][first : first + rows, :]
            at += rows


def rearrange(sources, parts):
    vmem = pl.BlockSpec(memory_space=pltpu.VMEM)
    return pl.pallas_call(
        functools.partial(copy_kernel, parts=parts),
        out_shape=[
            jax.ShapeDtypeStruct((sum(rows for _, _, rows in pieces), sources[0].shape[1]), bf16)
            for pieces in parts
        ],
        in_specs=[vmem] * len(sources),
        out_specs=[vmem] * len(parts),
        compiler_params=pltpu.CompilerParams(vmem_limit_bytes=20 * 1024 * 1024),
    )(*sources)


def ship(along_x, along_y, blocks):
    rows = along_x.shape[0]
    near = []
    for value, send in ((along_x, send_x), (along_y, send_y)):
        near += [value, send(value, 1), send(value, -1)]
    far = []
    for (below, above), send in ((near[1:3], send_x), (near[4:6], send_y)):
        far += [send(below[: rows // 2], 1), send(above[rows // 2 :], -1)]
    near, far, blocks = lax.optimization_barrier((near, far, blocks))
    lows_and_highs = rearrange(
        near + far,
        [
            pieces
            for turn in range(2)
            for pieces in (
                [(3 * turn, 0, rows), (3 * turn + 1, 0, rows)],
                [(3 * turn + 2, 0, rows)] + [(6 + 2 * turn + i, 0, rows // 2) for i in range(2)],
            )
        ],
    )
    sends = (send_y, send_y, send_x, send_x)
    steps = (1, -1, 1, -1)
    ub = lax.axis_size("ub")
    first = [send(value, step) for send, value, step in zip(sends, lows_and_highs, steps)]
    part = lax.all_to_all(blocks.reshape(ub, -1, blocks.shape[1]), "ub", 0, 0, tiled=True)
    first, lows_and_highs, part = lax.optimization_barrier((first, lows_and_highs, part))
    opposite = [send(value, step) for send, value, step in zip(sends, first, steps)]
    summed = everywhere(jnp.sum(part, axis=0), "ub").reshape(blocks.shape)
    opposite, lows_and_highs, summed = lax.optimization_barrier((opposite, lows_and_highs, summed))
    second = [send(value, -step) for send, value, step in zip(sends, lows_and_highs, steps)]
    shipped = []
    for turn in (slice(0, 2), slice(2, 4)):
        shipped += [*lows_and_highs[turn], *first[turn], *second[turn], *opposite[turn]]
    return shipped, summed


def per_device(user_factors, item_factors, tile_rows, tile_cols, tile_count, tile_weights):
    ub = lax.axis_size("ub")
    ib = lax.axis_size("ib")
    tile = tile_weights.shape[-1]
    slots = tile_rows.shape[-1]
    shard, full = user_factors.shape
    items = item_factors.shape[0]
    blocks = items // tile
    own = tile // ub
    user_total = shard * ub * ib
    me = lax.axis_index("ub")

    meta = jnp.concatenate(
        [tile_cols.reshape(-1), tile_count.reshape(1), jnp.zeros((tile - slots - 1,), jnp.int32)]
    ).astype(bf16)
    mine = tile_weights.reshape(slots, tile, ub, own).transpose(2, 0, 3, 1)
    mine = mine.reshape(ub, slots * own, tile)
    mine = jnp.concatenate([mine, jnp.broadcast_to(meta, (ub, 16, tile))], axis=1)
    got = lax.all_to_all(mine, "ub", 0, 0, tiled=True)

    held = shard // tile
    my_ib = lax.axis_index("ib")
    same_core, got = long_ring(user_factors.reshape(held, tile, full), got)
    wanted = tile_rows.reshape(slots)
    at_z, at_core = wanted // held // 2, wanted // held % 2
    spot = [0] * len(LONG_RING)
    for index, offset in enumerate(LONG_RING):
        spot[offset % len(LONG_RING)] = index
    order = jnp.array(spot, jnp.int32)[(at_z - my_ib // 2) % len(LONG_RING)]
    order = order + len(LONG_RING) * (at_core != my_ib % 2)
    near = same_core.reshape(-1, full)
    along_x, along_y, local = pick_tiles(
        order * held + wanted % held, near, send_core(near), tile=tile
    )
    shipped, local = ship(along_x, along_y, local)
    half = full // 2
    local = local * (UNOBSERVED / user_total)
    corner, across, last = jnp.split(local, 3, axis=0)
    gram = jnp.block([[corner, across], [across.T, last]])
    weights = got[:, : slots * own].reshape(ub * slots * own, tile).astype(f32)
    cols = got[:, slots * own, :slots].astype(jnp.int32)
    counts = got[:, slots * own, slots].astype(jnp.int32)

    own_items = lax.dynamic_slice_in_dim(
        item_factors.reshape(blocks, ub, own, full), me, 1, axis=1
    ).reshape(blocks * own, full)
    place = jnp.stack([me // GRID, me % GRID])
    result = solve(
        place, cols, counts, weights, gram, own_items, shipped, plan(slots), tile=tile, own=own
    )
    result = everywhere(result, "ub").reshape(ub, blocks, own, full)
    return result.transpose(1, 0, 2, 3).reshape(items, full)


def solution(mesh):
    in_specs = (
        P(("ub", "ib"), None),
        P("ib", None),
        P("ub", "ib", None),
        P("ub", "ib", None),
        P("ub", "ib"),
        P("ub", "ib", None, None, None),
    )
    return jax.shard_map(
        per_device, mesh=mesh, in_specs=in_specs, out_specs=P("ib", None), check_vma=False
    )
```
